32 devices in a mesh: groups: 2 (over x), seq: 16 (over z, y, core).
Axes of the slice: x: 2, y: 2, z: 4, core: 2. Of those that a mesh axis runs over, the one named last changes fastest.
Arguments:
- query: bfloat16 [4096, 1024], P(('groups', 'seq')), parts along dimension 0, may hold values from -6 to 6
- key: bfloat16 [4096, 1024], P(('groups', 'seq')), parts along dimension 0, may hold values from -6 to 6
- value: bfloat16 [4096, 1024], P(('groups', 'seq')), parts along dimension 0, may hold values from -6 to 6
- out_grad: bfloat16 [4096, 1024], P(('groups', 'seq')), parts along dimension 0, may hold values from -6 to 6
- session: int32 [4096], P('groups'), parts along dimension 0, may hold values from 0 to 7, never falling along the last dimension, each value on 1 to 512 neighbouring positions
Outputs:
- attended: bfloat16 [4096, 1024], P(('groups', 'seq')), parts along dimension 0
- query_grad: bfloat16 [4096, 1024], P(('groups', 'seq')), parts along dimension 0
- key_grad: bfloat16 [4096, 1024], P(('groups', 'seq')), parts along dimension 0
- value_grad: bfloat16 [4096, 1024], P(('groups', 'seq')), parts along dimension 0
The draws below stay inside these ranges and needn't reach their ends.
There are 2 independent parts, one for each index of `groups`. The reference program is written for one: setup_inputs(seed, part) draws one part's arguments, and reference() takes and returns one part's arrays. A program takes and returns all parts, laid end to end along the dimension named above; each array names one. Nothing has to cross between parts.
Inputs may be any that keep to these rules, and one draw needn't show every extreme that they name: session ids never fall along the packed order; each session holds 1 to 512 frames and one holds exactly 512.
All inputs are finite; a program needn't handle non-finite values.
Results may differ from the reference program's by a relative error of at most 0.023.
Values may be sent and summed in bfloat16 or wider, within the bound.
A program may use at most 64 MiB of HBM per device.

```python
import math
import jax
import jax.numpy as jnp
import numpy as np
from jax import lax

HEADS = 8
HEAD = 128
REACH = 4
TOK_DEV = 128
FEAT = 1024
TOKENS = 2048
SESSIONS = 8
N_SEQ = 16


def draw_query(key, part):
    key = jax.random.fold_in(key, 11)
    result = jnp.clip(jax.random.normal(key, (TOKENS, HEADS * HEAD)), -6.0, 6.0)
    return result.astype(jnp.bfloat16)


def draw_key(key, part):
    key = jax.random.fold_in(key, 23)
    result = jnp.clip(jax.random.normal(key, (TOKENS, HEADS * HEAD)), -6.0, 6.0)
    return result.astype(jnp.bfloat16)


def block_scale(rng, extent, split, low, top_value):
    level, own = 1.0, jax.random.fold_in(rng, 6)
    for axis_at, parts in split:
        draws = jnp.exp(jax.random.uniform(jax.random.fold_in(own, axis_at), (parts,), jnp.float32, low / len(split), top_value / len(split)))
        level = level * jnp.repeat(draws, extent[axis_at] // parts).reshape([-1 if axis == axis_at else 1 for axis in range(len(extent))])
    return level


def length_profile(number_of, total, limit, slope):
    weights = [(1 << 20) // math.isqrt(grade ** slope) + 1 for grade in range(2, number_of + 1)]
    spare, counts = total - limit - (number_of - 1), [1] * (number_of - 1)
    while spare > 0:
        movable = [i for i in range(number_of - 1) if counts[i] < limit]
        whole, left = sum([weights[i] for i in movable]), spare
        for i in movable:
            more = min(limit - counts[i], max(1, left * weights[i] // whole), spare)
            counts[i] = counts[i] + more
            spare = spare - more
    return np.array([limit] + counts)


def ragged(own_key, number_of, total, limit, skew):
    if number_of == 2:
        one = jax.random.randint(own_key, (), max(1, total - limit), min(limit, total - 1) + 1)
        return jnp.stack([one, total - one])
    lengths = jnp.asarray(length_profile(number_of, total, limit, skew), jnp.int32)
    couples = (number_of - 1) // 2
    donor, taker = lengths[1:1 + 2 * couples:2], lengths[2:2 + 2 * couples:2]
    room = jnp.minimum(donor - 1, limit - taker)
    moved = jax.random.randint(jax.random.fold_in(own_key, 1), (couples,), 0, 1 << 20) % (room + 1)
    lengths = lengths.at[1:1 + 2 * couples:2].set(donor - moved).at[2:2 + 2 * couples:2].set(taker + moved)
    return lengths[jax.random.permutation(jax.random.fold_in(own_key, 2), number_of)]


def noise(own_key, dims, width, limit, split=(), kind=jnp.bfloat16):
    gain = block_scale(own_key, dims, split, -0.22, 0.18) if split else 1.0
    array = jax.random.normal(own_key, dims, jnp.float32) * width * gain
    return jnp.minimum(jnp.maximum(array, -limit), limit).astype(kind)


def setup_inputs(seed: int = 0, part: int = 0) -> dict:
    seeds = jax.random.split(jax.random.key(seed), 6)
    part_keys = jax.random.split(jax.random.fold_in(seeds[5], part), 6)
    return {
        "query": draw_query(jax.random.fold_in(jax.random.fold_in(seeds[5], part), 71), part),
        "key": draw_key(jax.random.fold_in(jax.random.fold_in(seeds[5], part), 71), part),
        "value": noise(part_keys[2], (TOKENS, FEAT), 1.0, 6.0, ((0, 16),)),
        "out_grad": noise(part_keys[3], (TOKENS, FEAT), 1.0, 6.0, ((0, 16),)),
        "session": jnp.searchsorted(jnp.cumsum(ragged(part_keys[4], SESSIONS, TOKENS, REACH * TOK_DEV, 2)), jnp.arange(TOKENS), side="right").astype(jnp.int32),
    }


def split_heads(matrix):
    return matrix.astype(jnp.float32).reshape(matrix.shape[0], HEADS, HEAD)


def settle(matrix):
    return lax.optimization_barrier(matrix.astype(jnp.bfloat16))


def reference(query, key, value, out_grad, session):
    scaling = HEAD ** -0.5
    row_count = TOK_DEV
    features = HEADS * HEAD
    span = (2 * REACH + 1) * row_count
    margin = jnp.zeros((REACH * row_count, features), key.dtype)
    key_padded = jnp.concatenate([margin, key, margin], 0)
    value_padded = jnp.concatenate([margin, value, margin], 0)
    filler = jnp.full((REACH * row_count,), -1, jnp.int32)
    session_padded = jnp.concatenate([filler, session.astype(jnp.int32), filler])

    def one_block(carried, block_index):
        key_total, value_total = carried
        offset = (block_index * row_count).astype(jnp.int32)
        query_rows = split_heads(lax.dynamic_slice_in_dim(query, offset, row_count, 0))
        grad_rows = split_heads(lax.dynamic_slice_in_dim(out_grad, offset, row_count, 0))
        key_window = split_heads(lax.dynamic_slice_in_dim(key_padded, offset, span, 0))
        value_window = split_heads(lax.dynamic_slice_in_dim(value_padded, offset, span, 0))
        own_session = lax.dynamic_slice_in_dim(session.astype(jnp.int32), offset, row_count, 0)
        near_session = lax.dynamic_slice_in_dim(session_padded, offset, span, 0)
        matching = (own_session[:, None] == near_session[None, :])[None]
        raw_scores = jnp.einsum("qhd,khd->hqk", query_rows, key_window) * scaling
        scores = jnp.where(matching, raw_scores, -jnp.inf)
        highest = jnp.max(scores, axis=2, keepdims=True)
        log_total = highest + jnp.log(jnp.sum(jnp.exp(scores - highest), axis=2, keepdims=True))
        weights = jnp.exp(scores - log_total)
        probs = settle(weights).astype(jnp.float32)
        attended = jnp.einsum("hqk,khd->qhd", probs, value_window).reshape(row_count, features)
        attended = settle(attended)
        delta = jnp.einsum("qhd,qhd->hq", grad_rows, split_heads(attended))[:, :, None]
        grad_probs = jnp.einsum("qhd,khd->hqk", grad_rows, value_window)
        grad_scores = settle(weights * (grad_probs - delta) * scaling).astype(jnp.float32)
        query_grad = jnp.einsum("hqk,khd->qhd", grad_scores, key_window).reshape(row_count, features)
        key_part = jnp.einsum("hqk,qhd->khd", grad_scores, query_rows).reshape(span, features)
        value_part = jnp.einsum("hqk,qhd->khd", probs, grad_rows).reshape(span, features)
        key_total = lax.dynamic_update_slice_in_dim(
            key_total, lax.dynamic_slice_in_dim(key_total, offset, span, 0) + key_part, offset, 0)
        value_total = lax.dynamic_update_slice_in_dim(
            value_total, lax.dynamic_slice_in_dim(value_total, offset, span, 0) + value_part, offset, 0)
        return (key_total, value_total), (attended, query_grad.astype(jnp.bfloat16))

    empty = jnp.zeros((TOKENS + 2 * REACH * row_count, features), jnp.float32)
    totals, stacked = lax.scan(one_block, (empty, empty), jnp.arange(N_SEQ, dtype=jnp.int32))
    attended = stacked[0].reshape(TOKENS, features)
    query_grad = stacked[1].reshape(TOKENS, features)
    start = REACH * row_count
    key_grad = totals[0][start:start + TOKENS].astype(jnp.bfloat16)
    value_grad = totals[1][start:start + TOKENS].astype(jnp.bfloat16)
    return (attended, query_grad, key_grad, value_grad)
```

```python
import functools

import jax
import jax.numpy as jnp
from jax import lax
from jax.experimental import pallas as pl
from jax.experimental.pallas import tpu as pltpu
from jax.sharding import PartitionSpec as P

HEAD = 128
REACH = 4
ROWS = 128
PAIR = 2
TILE = 256
SCALING = HEAD ** (-0.5)
AWAY = -1e30
NOBODY = 127
BF = jnp.bfloat16
F32 = jnp.float32


def dot(left, right):
    return jnp.dot(left, right, preferred_element_type=F32)


def kernel(
    slabs,
    q_in, k_in, v_in, g_in, session,
    att_out, dq_out, dk_out, dv_out,
    kx, vw, qs, gs, qtx, gt, vt, kt, scores, acc,
    stage, arrived, small, final,
    own_sem, in_send, in_recv, z_send, z_recv, gz_send, gz_recv, out_own, out_send, out_recv,
):
    me = lax.axis_index("seq")
    slab, place = me // REACH, me % REACH
    side, core = place // 2, place % 2
    has_low, has_high = slab > 0, slab < slabs - 1

    def partner(d):
        return 2 * ((side + d // 2) % 2) + (core + d % 2) % 2

    def columns(of, h):
        return pl.ds(pl.multiple_of((PAIR * of + h) * HEAD, HEAD), HEAD)

    def remote(src, dst, send, recv, device):
        return pltpu.make_async_remote_copy(
            src_ref=src, dst_ref=dst, send_sem=send, recv_sem=recv,
            device_id={"seq": device}, device_id_type=pl.DeviceIdType.MESH,
        )

    def landing(t, h, block):
        if t == 0:
            return kx.at[h, block, :, pl.ds(0, HEAD)]
        return vw.at[h, block]

    def slab_landing(t, h, block):
        if t < 2:
            return landing(t, h, REACH + block)
        return (qs if t == 2 else gs).at[h, block]

    sources = (k_in, v_in, q_in, g_in)
    results = (att_out, dq_out, dk_out, dv_out)

    def in_copy(t, h, d, sending):
        other = partner(d)
        if sending:
            return remote(sources[t].at[:, columns(other, h)], slab_landing(t, h, place),
                          in_send.at[t, h, d - 1], in_recv.at[t, h, d - 1], slab * REACH + other)
        return remote(slab_landing(t, h, other), slab_landing(t, h, other),
                      in_send.at[t, h, d - 1], in_recv.at[t, h, d - 1], slab * REACH + other)

    def own_copy(t, h):
        return pltpu.make_async_copy(
            sources[t].at[:, columns(place, h)], slab_landing(t, h, place), own_sem.at[t, h])

    def z_copy(way, t, h, d):
        block = partner(d)
        src = sources[t].at[:, columns(place, h)] if d == 0 else landing(t, h, REACH + block)
        dst = landing(t, h, block + (2 * REACH if way == 0 else 0))
        return remote(src, dst, z_send.at[way, t, h, d], z_recv.at[way, t, h, d],
                      me + (-REACH if way == 0 else REACH))

    def gz_copy(way, h, part):
        return remote(stage.at[way, h, part], arrived.at[way, h, part],
                      gz_send.at[way, h, part], gz_recv.at[way, h, part],
                      me + (-REACH if way == 0 else REACH))

    def out_source(t, h, block):
        return small.at[t, h, block] if t < 2 else final.at[t - 2, h, block]

    def out_copy(t, h, d):
        other = partner(d)
        return remote(out_source(t, h, other), results[t].at[:, columns(place, h)],
                      out_send.at[t, h, d - 1], out_recv.at[t, h, d - 1], slab * REACH + other)

    def out_arrival(t, h, d):
        other = partner(d)
        dst = results[t].at[:, columns(other, h)]
        return remote(out_source(t, h, other), dst,
                      out_send.at[t, h, d - 1], out_recv.at[t, h, d - 1], slab * REACH + other)

    def out_own_copy(t, h):
        return pltpu.make_async_copy(
            out_source(t, h, place), results[t].at[:, columns(place, h)], out_own.at[t, h])

    def both_ways(action):
        @pl.when(has_low)
        def _():
            action(0)

        @pl.when(has_high)
        def _():
            action(1)

    barrier = pltpu.get_barrier_semaphore()
    for d in (1, 2, 3):
        pl.semaphore_signal(barrier, inc=1, device_id={"seq": slab * REACH + partner(d)},
                            device_id_type=pl.DeviceIdType.MESH)

    def greet(way):
        pl.semaphore_signal(barrier, inc=1, device_id={"seq": me + (-REACH if way == 0 else REACH)},
                            device_id_type=pl.DeviceIdType.MESH)

    both_ways(greet)
    for h in range(PAIR):
        for t in (0, 1, 2, 3):
            own_copy(t, h).start()
    pl.semaphore_wait(barrier, 3 + has_low.astype(jnp.int32) + has_high.astype(jnp.int32))

    for h in range(PAIR):
        for d in (2, 3, 1):
            for t in (0, 1):
                in_copy(t, h, d, True).start()
        for t in (0, 1):
            both_ways(lambda way: z_copy(way, t, h, 0).start())
        for d in (2, 3, 1):
            for t in (2, 3):
                in_copy(t, h, d, True).start()

    rows = lax.broadcasted_iota(jnp.int32, (ROWS, ROWS), 0)
    for w in range(3 * REACH):
        block = slab * REACH - REACH + w
        inside = jnp.logical_and(block >= 0, block < slabs * REACH)
        held = session[pl.ds(jnp.clip(block, 0, slabs * REACH - 1), 1), :]
        held = jnp.where(inside, held, NOBODY)
        hot = jnp.where(rows == held, 1.0, 0.0).astype(F32).T.astype(BF)
        for h in range(PAIR):
            kx[h, w, :, HEAD:] = hot
    for block in range(REACH):
        held = session[pl.ds(slab * REACH + block, 1), :]
        away = jnp.where(rows == held, 0.0, AWAY).astype(BF)
        at = (block % 2) * ROWS
        for h in range(PAIR):
            qtx[h, block // 2, HEAD:, at:at + ROWS] = away
    acc[...] = jnp.zeros_like(acc)

    def empty(way):
        first = 0 if way == 0 else 2 * REACH
        zeros = jnp.zeros((PAIR, REACH, ROWS, HEAD), BF)
        kx[:, first:first + REACH, :, :HEAD] = zeros
        vw[:, first:first + REACH] = zeros
        arrived[1 - way] = jnp.zeros(arrived.shape[1:], BF)

    pl.when(jnp.logical_not(has_low))(lambda: empty(0))
    pl.when(jnp.logical_not(has_high))(lambda: empty(1))

    for h in range(PAIR):
        for d in (1, 2, 3):
            for t in (0, 1):
                in_copy(t, h, d, False).wait_recv()
                both_ways(lambda way: z_copy(way, t, h, d).start())

    def chunk(h, c):
        q = qs[h, 2 * c:2 * c + 2].reshape(TILE, HEAD)
        g = gs[h, 2 * c:2 * c + 2].reshape(TILE, HEAD)
        g_t = gt[c]
        high = None
        for i in range(5):
            w = 2 * (c + i)
            s = dot(kx[h, w:w + 2].reshape(TILE, 2 * HEAD), qtx[h, c])
            scores[i] = s
            top = jnp.max(s, axis=0, keepdims=True)
            high = top if high is None else jnp.maximum(high, top)
        total = jnp.zeros((1, TILE), F32)
        for i in range(5):
            e = jnp.exp((scores[i] - high) * SCALING)
            scores[i] = e
            total = total + jnp.sum(e, axis=0, keepdims=True)
        share = 1.0 / total
        att = jnp.zeros((HEAD, TILE), F32)
        for i in range(5):
            p = scores[i] * share
            scores[i] = p
            p = p.astype(BF)
            att = att + dot(vt[c + i], p)
            acc[h, c + i, 1] += dot(p, g)
        att = att.astype(BF).astype(F32)
        delta = jnp.sum(g_t.astype(F32) * att, axis=0, keepdims=True)
        small[0, h, 2 * c:2 * c + 2] = att.T.astype(BF).reshape(2, ROWS, HEAD)
        dq = jnp.zeros((HEAD, TILE), F32)
        for i in range(5):
            w = 2 * (c + i)
            dp = dot(vw[h, w:w + 2].reshape(TILE, HEAD), g_t)
            ds = (scores[i] * (dp - delta) * SCALING).astype(BF)
            dq = dq + dot(kt[c + i], ds)
            acc[h, c + i, 0] += dot(ds, q)
        small[1, h, 2 * c:2 * c + 2] = dq.T.astype(BF).reshape(2, ROWS, HEAD)

    def finish(h):
        for part in range(2):
            pl.when(has_high)(lambda: gz_copy(0, h, part).wait_recv())
            pl.when(has_low)(lambda: gz_copy(1, h, part).wait_recv())
            for t in range(2):
                whole = (acc[h, 2 + part, t] + arrived[0, h, part, t].astype(F32)
                         + arrived[1, h, part, t].astype(F32))
                final[t, h, 2 * part:2 * part + 2] = whole.astype(BF).reshape(2, ROWS, HEAD)
        for t in (2, 3):
            for d in (2, 3, 1):
                out_copy(t, h, d).start()
            out_own_copy(t, h).start()

    def head(h, carry):
        for t in range(4):
            own_copy(t, h).wait()
            if t >= 2:
                for d in (1, 2, 3):
                    in_copy(t, h, d, False).wait_recv()
        for c in range(2):
            at = slice(2 * c, 2 * c + 2)
            qtx[h, c, :HEAD] = qs[h, at].reshape(TILE, HEAD).T
            gt[c] = gs[h, at].reshape(TILE, HEAD).T

        def window_arrival(way):
            for t in range(2):
                for d in range(4):
                    block = partner(d) + (0 if way == 0 else 2 * REACH)
                    remote(landing(t, h, block), landing(t, h, block), z_send.at[1 - way, t, h, d],
                           z_recv.at[1 - way, t, h, d], me + (-REACH if way == 0 else REACH)).wait_recv()

        both_ways(window_arrival)
        for i in range(6):
            vt[i] = vw[h, 2 * i:2 * i + 2].reshape(TILE, HEAD).T
            kt[i] = kx[h, 2 * i:2 * i + 2, :, :HEAD].reshape(TILE, HEAD).T
        chunk(h, 0)
        stage[0, h, 0] = acc[h, 0].astype(BF)
        pl.when(has_low)(lambda: gz_copy(0, h, 0).start())
        pl.when(h == 1)(lambda: finish(0))
        chunk(h, 1)
        stage[0, h, 1] = acc[h, 1].astype(BF)
        pl.when(has_low)(lambda: gz_copy(0, h, 1).start())
        for part in range(2):
            stage[1, h, part] = acc[h, 4 + part].astype(BF)
            pl.when(has_high)(lambda: gz_copy(1, h, part).start())
        for t in range(2):
            for d in (2, 3, 1):
                out_copy(t, h, d).start()
            out_own_copy(t, h).start()
        return carry

    lax.fori_loop(0, PAIR, head, 0)
    finish(1)

    for h in range(PAIR):
        for t in range(4):
            for d in (1, 2, 3):
                in_copy(t, h, d, True).wait_send()
                out_copy(t, h, d).wait_send()
                out_arrival(t, h, d).wait_recv()
            out_own_copy(t, h).wait()

        def sent(way):
            for t in range(2):
                for d in range(4):
                    z_copy(way, t, h, d).wait_send()
            for part in range(2):
                gz_copy(way, h, part).wait_send()

        both_ways(sent)


def shards(slabs, query, key, value, out_grad, session):
    rows, features = query.shape
    dma = pltpu.SemaphoreType.DMA
    result = jax.ShapeDtypeStruct((rows, features), BF)
    return pl.pallas_call(
        functools.partial(kernel, slabs),
        out_shape=(result,) * 4,
        in_specs=[pl.BlockSpec(memory_space=pl.ANY)] * 4 + [pl.BlockSpec(memory_space=pltpu.VMEM)],
        out_specs=(pl.BlockSpec(memory_space=pl.ANY),) * 4,
        scratch_shapes=[
            pltpu.VMEM((PAIR, 3 * REACH, ROWS, 2 * HEAD), BF),
            pltpu.VMEM((PAIR, 3 * REACH, ROWS, HEAD), BF),
            pltpu.VMEM((PAIR, REACH, ROWS, HEAD), BF),
            pltpu.VMEM((PAIR, REACH, ROWS, HEAD), BF),
            pltpu.VMEM((PAIR, 2, 2 * HEAD, TILE), BF),
            pltpu.VMEM((2, HEAD, TILE), BF),
            pltpu.VMEM((6, HEAD, TILE), BF),
            pltpu.VMEM((6, HEAD, TILE), BF),
            pltpu.VMEM((5, TILE, TILE), F32),
            pltpu.VMEM((PAIR, 6, 2, TILE, HEAD), F32),
            pltpu.VMEM((2, PAIR, 2, 2, TILE, HEAD), BF),
            pltpu.VMEM((2, PAIR, 2, 2, TILE, HEAD), BF),
            pltpu.VMEM((2, PAIR, REACH, ROWS, HEAD), BF),
            pltpu.VMEM((2, PAIR, REACH, ROWS, HEAD), BF),
            dma((4, PAIR)),
            dma((4, PAIR, 3)),
            dma((4, PAIR, 3)),
            dma((2, 2, PAIR, 4)),
            dma((2, 2, PAIR, 4)),
            dma((2, PAIR, 2)),
            dma((2, PAIR, 2)),
            dma((4, PAIR)),
            dma((4, PAIR, 3)),
            dma((4, PAIR, 3)),
        ],
        compiler_params=pltpu.CompilerParams(
            collective_id=0, has_side_effects=True, vmem_limit_bytes=40 * 1024 * 1024),
        cost_estimate=pl.CostEstimate(
            flops=2_000_000_000, bytes_accessed=2_100_000, transcendentals=1_300_000),
    )(query, key, value, out_grad, session.reshape(-1, ROWS))


def solution(mesh):
    split = P(("groups", "seq"), None)
    return jax.shard_map(
        functools.partial(shards, mesh.shape["seq"] // REACH),
        mesh=mesh,
        in_specs=(split, split, split, split, P("groups")),
        out_specs=(split,) * 4,
        check_vma=False,
    )
```

```python
import functools

import jax
import jax.numpy as jnp
from jax import lax
from jax.experimental import pallas as pl
from jax.experimental.pallas import tpu as pltpu
from jax.sharding import PartitionSpec as P

HEAD = 128
REACH = 4
ROWS = 128
PAIR = 2
TILE = 256
SCALING = HEAD ** (-0.5)
AWAY = -1e30
NOBODY = 127
BF = jnp.bfloat16
F32 = jnp.float32


def dot(left, right):
    return jnp.dot(left, right, preferred_element_type=F32)


def kernel(
    slabs,
    q_in, k_in, v_in, g_in, session,
    att_out, dq_out, dk_out, dv_out,
    kx, vw, qs, gs, qtx, gt, vt, kt, scores, acc,
    stage, arrived, small, final,
    own_sem, in_send, in_recv, z_send, z_recv, gz_send, gz_recv, out_own, out_send, out_recv,
):
    me = lax.axis_index("seq")
    slab, place = me // REACH, me % REACH
    side, core = place // 2, place % 2
    has_low, has_high = slab > 0, slab < slabs - 1

    def partner(d):
        return 2 * ((side + d // 2) % 2) + (core + d % 2) % 2

    def columns(of, h):
        return pl.ds(pl.multiple_of((PAIR * of + h) * HEAD, HEAD), HEAD)

    def remote(src, dst, send, recv, device):
        return pltpu.make_async_remote_copy(
            src_ref=src, dst_ref=dst, send_sem=send, recv_sem=recv,
            device_id={"seq": device}, device_id_type=pl.DeviceIdType.MESH,
        )

    def landing(t, h, block):
        if t == 0:
            return kx.at[h, block, :, pl.ds(0, HEAD)]
        return vw.at[h, block]

    def slab_landing(t, h, block):
        if t < 2:
            return landing(t, h, REACH + block)
        return (qs if t == 2 else gs).at[h, block]

    sources = (k_in, v_in, q_in, g_in)
    results = (att_out, dq_out, dk_out, dv_out)

    def in_copy(t, h, d, sending):
        other = partner(d)
        if sending:
            return remote(sources[t].at[:, columns(other, h)], slab_landing(t, h, place),
                          in_send.at[t, h, d - 1], in_recv.at[t, h, d - 1], slab * REACH + other)
        return remote(slab_landing(t, h, other), slab_landing(t, h, other),
                      in_send.at[t, h, d - 1], in_recv.at[t, h, d - 1], slab * REACH + other)

    def own_copy(t, h):
        return pltpu.make_async_copy(
            sources[t].at[:, columns(place, h)], slab_landing(t, h, place), own_sem.at[t, h])

    def z_copy(way, t, h, d):
        block = partner(d)
        src = sources[t].at[:, columns(place, h)] if d == 0 else landing(t, h, REACH + block)
        dst = landing(t, h, block + (2 * REACH if way == 0 else 0))
        return remote(src, dst, z_send.at[way, t, h, d], z_recv.at[way, t, h, d],
                      me + (-REACH if way == 0 else REACH))

    def gz_copy(way, h, part):
        return remote(stage.at[way, h, part], arrived.at[way, h, part],
                      gz_send.at[way, h, part], gz_recv.at[way, h, part],
                      me + (-REACH if way == 0 else REACH))

    def out_source(t, h, block):
        return small.at[t, h, block] if t < 2 else final.at[t - 2, h, block]

    def out_copy(t, h, d):
        other = partner(d)
        return remote(out_source(t, h, other), results[t].at[:, columns(place, h)],
                      out_send.at[t, h, d - 1], out_recv.at[t, h, d - 1], slab * REACH + other)

    def out_arrival(t, h, d):
        other = partner(d)
        dst = results[t].at[:, columns(other, h)]
        return remote(out_source(t, h, other), dst,
                      out_send.at[t, h, d - 1], out_recv.at[t, h, d - 1], slab * REACH + other)

    def out_own_copy(t, h):
        return pltpu.make_async_copy(
            out_source(t, h, place), results[t].at[:, columns(place, h)], out_own.at[t, h])

    def both_ways(action):
        @pl.when(has_low)
        def _():
            action(0)

        @pl.when(has_high)
        def _():
            action(1)

    barrier = pltpu.get_barrier_semaphore()
    for d in (1, 2, 3):
        pl.semaphore_signal(barrier, inc=1, device_id={"seq": slab * REACH + partner(d)},
                            device_id_type=pl.DeviceIdType.MESH)

    def greet(way):
        pl.semaphore_signal(barrier, inc=1, device_id={"seq": me + (-REACH if way == 0 else REACH)},
                            device_id_type=pl.DeviceIdType.MESH)

    both_ways(greet)
    for h in range(PAIR):
        for t in (0, 1, 2, 3):
            own_copy(t, h).start()
    pl.semaphore_wait(barrier, 3 + has_low.astype(jnp.int32) + has_high.astype(jnp.int32))

    def send_inputs(h):
        for d in (2, 3):
            for t in (0, 1):
                in_copy(t, h, d, True).start()
        for t in (0, 1):
            in_copy(t, h, 1, True).start()
            both_ways(lambda way: z_copy(way, t, h, 0).start())
        for d in (2, 3, 1):
            for t in (2, 3):
                in_copy(t, h, d, True).start()

    def relay(h, d):
        for t in (0, 1):
            in_copy(t, h, d, False).wait_recv()
            both_ways(lambda way: z_copy(way, t, h, d).start())

    send_inputs(0)

    rows = lax.broadcasted_iota(jnp.int32, (ROWS, ROWS), 0)
    for w in range(3 * REACH):
        block = slab * REACH - REACH + w
        inside = jnp.logical_and(block >= 0, block < slabs * REACH)
        held = session[pl.ds(jnp.clip(block, 0, slabs * REACH - 1), 1), :]
        held = jnp.where(inside, held, NOBODY)
        hot = jnp.where(rows == held, 1.0, 0.0).astype(F32).T.astype(BF)
        for h in range(PAIR):
            kx[h, w, :, HEAD:] = hot
    for block in range(REACH):
        held = session[pl.ds(slab * REACH + block, 1), :]
        away = jnp.where(rows == held, 0.0, AWAY).astype(BF)
        at = (block % 2) * ROWS
        for h in range(PAIR):
            qtx[h, block // 2, HEAD:, at:at + ROWS] = away
    def empty(way):
        first = 0 if way == 0 else 2 * REACH
        zeros = jnp.zeros((PAIR, REACH, ROWS, HEAD), BF)
        kx[:, first:first + REACH, :, :HEAD] = zeros
        vw[:, first:first + REACH] = zeros
        arrived[1 - way] = jnp.zeros(arrived.shape[1:], BF)

    pl.when(jnp.logical_not(has_low))(lambda: empty(0))
    pl.when(jnp.logical_not(has_high))(lambda: empty(1))

    for d in (1, 2, 3):
        relay(0, d)
    send_inputs(1)
    relay(1, 1)
    acc[...] = jnp.zeros_like(acc)

    def chunk(h, c):
        q = qs[h, 2 * c:2 * c + 2].reshape(TILE, HEAD)
        g = gs[h, 2 * c:2 * c + 2].reshape(TILE, HEAD)
        g_t = gt[c]
        high = None
        for i in range(5):
            w = 2 * (c + i)
            s = dot(kx[h, w:w + 2].reshape(TILE, 2 * HEAD), qtx[h, c])
            scores[i] = s
            top = jnp.max(s, axis=0, keepdims=True)
            high = top if high is None else jnp.maximum(high, top)
        total = jnp.zeros((1, TILE), F32)
        for i in range(5):
            e = jnp.exp((scores[i] - high) * SCALING)
            scores[i] = e
            total = total + jnp.sum(e, axis=0, keepdims=True)
        share = 1.0 / total
        att = jnp.zeros((HEAD, TILE), F32)
        for i in range(5):
            p = scores[i] * share
            scores[i] = p
            p = p.astype(BF)
            att = att + dot(vt[c + i], p)
            acc[h, c + i, 1] += dot(p, g)
        att = att.astype(BF).astype(F32)
        delta = jnp.sum(g_t.astype(F32) * att, axis=0, keepdims=True)
        small[0, h, 2 * c:2 * c + 2] = att.T.astype(BF).reshape(2, ROWS, HEAD)
        dq = jnp.zeros((HEAD, TILE), F32)
        for i in range(5):
            w = 2 * (c + i)
            dp = dot(vw[h, w:w + 2].reshape(TILE, HEAD), g_t)
            ds = (scores[i] * (dp - delta) * SCALING).astype(BF)
            dq = dq + dot(kt[c + i], ds)
            acc[h, c + i, 0] += dot(ds, q)
        small[1, h, 2 * c:2 * c + 2] = dq.T.astype(BF).reshape(2, ROWS, HEAD)

    def finish(h):
        for part in range(2):
            pl.when(has_high)(lambda: gz_copy(0, h, part).wait_recv())
            pl.when(has_low)(lambda: gz_copy(1, h, part).wait_recv())
            for t in range(2):
                whole = (acc[h, 2 + part, t] + arrived[0, h, part, t].astype(F32)
                         + arrived[1, h, part, t].astype(F32))
                final[t, h, 2 * part:2 * part + 2] = whole.astype(BF).reshape(2, ROWS, HEAD)

            @pl.when(side == part)
            def _():
                for t in (2, 3):
                    out_copy(t, h, 1).start()
                    out_own_copy(t, h).start()

            @pl.when(side != part)
            def _():
                for t in (2, 3):
                    out_copy(t, h, 2).start()
                    out_copy(t, h, 3).start()

    def head(h, carry):
        for t in range(4):
            own_copy(t, h).wait()
            if t >= 2:
                for d in (1, 2, 3):
                    in_copy(t, h, d, False).wait_recv()
        for c in range(2):
            at = slice(2 * c, 2 * c + 2)
            qtx[h, c, :HEAD] = qs[h, at].reshape(TILE, HEAD).T
            gt[c] = gs[h, at].reshape(TILE, HEAD).T

        def window_arrival(way):
            for t in range(2):
                for d in range(4):
                    block = partner(d) + (0 if way == 0 else 2 * REACH)
                    remote(landing(t, h, block), landing(t, h, block), z_send.at[1 - way, t, h, d],
                           z_recv.at[1 - way, t, h, d], me + (-REACH if way == 0 else REACH)).wait_recv()

        def turned(i):
            vt[i] = vw[h, 2 * i:2 * i + 2].reshape(TILE, HEAD).T
            kt[i] = kx[h, 2 * i:2 * i + 2, :, :HEAD].reshape(TILE, HEAD).T

        turned(2)
        turned(3)
        both_ways(window_arrival)
        for i in (0, 1, 4, 5):
            turned(i)
        chunk(h, 0)
        stage[0, h, 0] = acc[h, 0].astype(BF)
        pl.when(has_low)(lambda: gz_copy(0, h, 0).start())

        @pl.when(h == 0)
        def _():
            relay(1, 2)
            relay(1, 3)

        chunk(h, 1)
        stage[0, h, 1] = acc[h, 1].astype(BF)
        pl.when(has_low)(lambda: gz_copy(0, h, 1).start())
        for part in range(2):
            stage[1, h, part] = acc[h, 4 + part].astype(BF)
            pl.when(has_high)(lambda: gz_copy(1, h, part).start())
        for t in range(2):
            for d in (2, 3, 1):
                out_copy(t, h, d).start()
            out_own_copy(t, h).start()
        return carry

    lax.fori_loop(0, PAIR, head, 0)

    for h in range(PAIR):
        for t in range(4):
            for d in (1, 2, 3):
                in_copy(t, h, d, True).wait_send()

        def sent(way):
            for t in range(2):
                for d in range(4):
                    z_copy(way, t, h, d).wait_send()

        both_ways(sent)

    finish(0)
    finish(1)
    for h in range(PAIR):
        both_ways(lambda way: [gz_copy(way, h, part).wait_send() for part in range(2)] and None)
        for t in range(4):
            out_own_copy(t, h).wait()
            for d in (1, 2, 3):
                out_copy(t, h, d).wait_send()
                out_arrival(t, h, d).wait_recv()


def hand_over(*refs):
    sources, results, sems = refs[:4], refs[4:8], refs[8]
    copies = [pltpu.make_async_copy(sources[t], results[t], sems.at[t]) for t in range(4)]
    for copy in copies:
        copy.start()
    for copy in copies:
        copy.wait()


def shards(slabs, query, key, value, out_grad, session):
    rows, features = query.shape
    dma = pltpu.SemaphoreType.DMA
    result = jax.ShapeDtypeStruct((rows, features), BF)
    done = pl.pallas_call(
        functools.partial(kernel, slabs),
        out_shape=(result,) * 4,
        in_specs=[pl.BlockSpec(memory_space=pltpu.HBM)] * 4 + [pl.BlockSpec(memory_space=pltpu.VMEM)],
        out_specs=(pl.BlockSpec(memory_space=pl.ANY),) * 4,
        scratch_shapes=[
            pltpu.VMEM((PAIR, 3 * REACH, ROWS, 2 * HEAD), BF),
            pltpu.VMEM((PAIR, 3 * REACH, ROWS, HEAD), BF),
            pltpu.VMEM((PAIR, REACH, ROWS, HEAD), BF),
            pltpu.VMEM((PAIR, REACH, ROWS, HEAD), BF),
            pltpu.VMEM((PAIR, 2, 2 * HEAD, TILE), BF),
            pltpu.VMEM((2, HEAD, TILE), BF),
            pltpu.VMEM((6, HEAD, TILE), BF),
            pltpu.VMEM((6, HEAD, TILE), BF),
            pltpu.VMEM((5, TILE, TILE), F32),
            pltpu.VMEM((PAIR, 6, 2, TILE, HEAD), F32),
            pltpu.VMEM((2, PAIR, 2, 2, TILE, HEAD), BF),
            pltpu.VMEM((2, PAIR, 2, 2, TILE, HEAD), BF),
            pltpu.VMEM((2, PAIR, REACH, ROWS, HEAD), BF),
            pltpu.VMEM((2, PAIR, REACH, ROWS, HEAD), BF),
            dma((4, PAIR)),
            dma((4, PAIR, 3)),
            dma((4, PAIR, 3)),
            dma((2, 2, PAIR, 4)),
            dma((2, 2, PAIR, 4)),
            dma((2, PAIR, 2)),
            dma((2, PAIR, 2)),
            dma((4, PAIR)),
            dma((4, PAIR, 3)),
            dma((4, PAIR, 3)),
        ],
        compiler_params=pltpu.CompilerParams(
            collective_id=0, has_side_effects=True, vmem_limit_bytes=62 * 1024 * 1024),
        cost_estimate=pl.CostEstimate(
            flops=2_000_000_000, bytes_accessed=2_100_000, transcendentals=1_300_000),
    )(query, key, value, out_grad, session.reshape(-1, ROWS))
    return pl.pallas_call(
        hand_over,
        out_shape=(result,) * 4,
        in_specs=[pl.BlockSpec(memory_space=pltpu.VMEM)] * 4,
        out_specs=(pl.BlockSpec(memory_space=pltpu.HBM),) * 4,
        scratch_shapes=[dma((4,))],
        compiler_params=pltpu.CompilerParams(vmem_limit_bytes=62 * 1024 * 1024),
    )(*done)


def solution(mesh):
    split = P(("groups", "seq"), None)
    return jax.shard_map(
        functools.partial(shards, mesh.shape["seq"] // REACH),
        mesh=mesh,
        in_specs=(split, split, split, split, P("groups")),
        out_specs=(split,) * 4,
        check_vma=False,
    )
```

```python
import functools

import jax
import jax.numpy as jnp
from jax import lax
from jax.experimental import pallas as pl
from jax.experimental.pallas import tpu as pltpu
from jax.sharding import PartitionSpec as P

HEAD = 128
REACH = 4
ROWS = 128
PAIR = 2
TILE = 256
SCALING = HEAD ** (-0.5)
AWAY = -1e30
NOBODY = 127
BF = jnp.bfloat16
F32 = jnp.float32


def dot(left, right):
    return jnp.dot(left, right, preferred_element_type=F32)


def kernel(
    slabs,
    q_in, k_in, v_in, g_in, session,
    att_out, dq_out, dk_out, dv_out,
    kx, vw, qs, gs, qtx, gt, vt, kt, scores, acc,
    stage, arrived, small, final,
    own_sem, in_send, in_recv, z_send, z_recv, gz_send, gz_recv, out_own, out_send, out_recv,
):
    me = lax.axis_index("seq")
    slab, place = me // REACH, me % REACH
    side, core = place // 2, place % 2
    has_low, has_high = slab > 0, slab < slabs - 1

    def partner(d):
        return 2 * ((side + d // 2) % 2) + (core + d % 2) % 2

    def columns(of, h):
        return pl.ds(pl.multiple_of((PAIR * of + h) * HEAD, HEAD), HEAD)

    def remote(src, dst, send, recv, device):
        return pltpu.make_async_remote_copy(
            src_ref=src, dst_ref=dst, send_sem=send, recv_sem=recv,
            device_id={"seq": device}, device_id_type=pl.DeviceIdType.MESH,
        )

    def landing(t, h, block):
        if t == 0:
            return kx.at[h, block, :, pl.ds(0, HEAD)]
        return vw.at[h, block]

    def slab_landing(t, h, block):
        if t < 2:
            return landing(t, h, REACH + block)
        return (qs if t == 2 else gs).at[h, block]

    sources = (k_in, v_in, q_in, g_in)
    results = (att_out, dq_out, dk_out, dv_out)

    def in_copy(t, h, d, sending):
        other = partner(d)
        if sending:
            return remote(sources[t].at[:, columns(other, h)], slab_landing(t, h, place),
                          in_send.at[t, h, d - 1], in_recv.at[t, h, d - 1], slab * REACH + other)
        return remote(slab_landing(t, h, other), slab_landing(t, h, other),
                      in_send.at[t, h, d - 1], in_recv.at[t, h, d - 1], slab * REACH + other)

    def own_copy(t, h):
        return pltpu.make_async_copy(
            sources[t].at[:, columns(place, h)], slab_landing(t, h, place), own_sem.at[t, h])

    def z_copy(way, t, h, d):
        block = partner(d)
        src = sources[t].at[:, columns(place, h)] if d == 0 else landing(t, h, REACH + block)
        dst = landing(t, h, block + (2 * REACH if way == 0 else 0))
        return remote(src, dst, z_send.at[way, t, h, d], z_recv.at[way, t, h, d],
                      me + (-REACH if way == 0 else REACH))

    def gz_copy(way, h, part):
        return remote(stage.at[way, h, part], arrived.at[way, h, part],
                      gz_send.at[way, h, part], gz_recv.at[way, h, part],
                      me + (-REACH if way == 0 else REACH))

    def out_source(t, h, block):
        return small.at[t, h, block] if t < 2 else final.at[t - 2, h, block]

    def out_copy(t, h, d):
        other = partner(d)
        return remote(out_source(t, h, other), results[t].at[:, columns(place, h)],
                      out_send.at[t, h, d - 1], out_recv.at[t, h, d - 1], slab * REACH + other)

    def out_arrival(t, h, d):
        other = partner(d)
        dst = results[t].at[:, columns(other, h)]
        return remote(out_source(t, h, other), dst,
                      out_send.at[t, h, d - 1], out_recv.at[t, h, d - 1], slab * REACH + other)

    def out_own_copy(t, h):
        return pltpu.make_async_copy(
            out_source(t, h, place), results[t].at[:, columns(place, h)], out_own.at[t, h])

    def both_ways(action):
        @pl.when(has_low)
        def _():
            action(0)

        @pl.when(has_high)
        def _():
            action(1)

    barrier = pltpu.get_barrier_semaphore()
    for d in (1, 2, 3):
        pl.semaphore_signal(barrier, inc=1, device_id={"seq": slab * REACH + partner(d)},
                            device_id_type=pl.DeviceIdType.MESH)

    def greet(way):
        pl.semaphore_signal(barrier, inc=1, device_id={"seq": me + (-REACH if way == 0 else REACH)},
                            device_id_type=pl.DeviceIdType.MESH)

    both_ways(greet)
    for h in range(PAIR):
        for t in (0, 1, 2, 3):
            own_copy(t, h).start()
    pl.semaphore_wait(barrier, 3 + has_low.astype(jnp.int32) + has_high.astype(jnp.int32))

    def send_inputs(h):
        for d in (2, 3):
            for t in (0, 1):
                in_copy(t, h, d, True).start()
        for t in (0, 1):
            in_copy(t, h, 1, True).start()
            both_ways(lambda way: z_copy(way, t, h, 0).start())
        for d in (2, 3, 1):
            for t in (2, 3):
                in_copy(t, h, d, True).start()

    def relay(h, d):
        for t in (0, 1):
            in_copy(t, h, d, False).wait_recv()
            both_ways(lambda way: z_copy(way, t, h, d).start())

    send_inputs(0)

    rows = lax.broadcasted_iota(jnp.int32, (ROWS, ROWS), 0)
    for w in range(3 * REACH):
        block = slab * REACH - REACH + w
        inside = jnp.logical_and(block >= 0, block < slabs * REACH)
        held = session[pl.ds(jnp.clip(block, 0, slabs * REACH - 1), 1), :]
        held = jnp.where(inside, held, NOBODY)
        hot = jnp.where(rows == held, 1.0, 0.0).astype(F32).T.astype(BF)
        for h in range(PAIR):
            kx[h, w, :, HEAD:] = hot
    for block in range(REACH):
        held = session[pl.ds(slab * REACH + block, 1), :]
        away = jnp.where(rows == held, 0.0, AWAY).astype(BF)
        at = (block % 2) * ROWS
        for h in range(PAIR):
            qtx[h, block // 2, HEAD:, at:at + ROWS] = away
    def empty(way):
        first = 0 if way == 0 else 2 * REACH
        zeros = jnp.zeros((PAIR, REACH, ROWS, HEAD), BF)
        kx[:, first:first + REACH, :, :HEAD] = zeros
        vw[:, first:first + REACH] = zeros
        arrived[1 - way] = jnp.zeros(arrived.shape[1:], BF)

    pl.when(jnp.logical_not(has_low))(lambda: empty(0))
    pl.when(jnp.logical_not(has_high))(lambda: empty(1))

    for d in (1, 2, 3):
        relay(0, d)
    send_inputs(1)
    relay(1, 1)
    acc[...] = jnp.zeros_like(acc)

    def chunk(h, c, between=lambda: None):
        q = qs[h, 2 * c:2 * c + 2].reshape(TILE, HEAD)
        g = gs[h, 2 * c:2 * c + 2].reshape(TILE, HEAD)
        g_t = gt[c]
        high = None
        for i in range(5):
            w = 2 * (c + i)
            s = dot(kx[h, w:w + 2].reshape(TILE, 2 * HEAD), qtx[h, c])
            scores[i] = s
            top = jnp.max(s, axis=0, keepdims=True)
            high = top if high is None else jnp.maximum(high, top)
        total = jnp.zeros((1, TILE), F32)
        for i in range(5):
            e = jnp.exp((scores[i] - high) * SCALING)
            scores[i] = e
            total = total + jnp.sum(e, axis=0, keepdims=True)
        between()
        share = 1.0 / total
        att = jnp.zeros((HEAD, TILE), F32)
        for i in range(5):
            p = scores[i] * share
            scores[i] = p
            p = p.astype(BF)
            att = att + dot(vt[c + i], p)
            acc[h, c + i, 1] += dot(p, g)
        att = att.astype(BF).astype(F32)
        delta = jnp.sum(g_t.astype(F32) * att, axis=0, keepdims=True)
        small[0, h, 2 * c:2 * c + 2] = att.T.astype(BF).reshape(2, ROWS, HEAD)
        dq = jnp.zeros((HEAD, TILE), F32)
        for i in range(5):
            w = 2 * (c + i)
            dp = dot(vw[h, w:w + 2].reshape(TILE, HEAD), g_t)
            ds = (scores[i] * (dp - delta) * SCALING).astype(BF)
            dq = dq + dot(kt[c + i], ds)
            acc[h, c + i, 0] += dot(ds, q)
        small[1, h, 2 * c:2 * c + 2] = dq.T.astype(BF).reshape(2, ROWS, HEAD)

    def finish(h):
        for part in range(2):
            pl.when(has_high)(lambda: gz_copy(0, h, part).wait_recv())
            pl.when(has_low)(lambda: gz_copy(1, h, part).wait_recv())
            for t in range(2):
                whole = (acc[h, 2 + part, t] + arrived[0, h, part, t].astype(F32)
                         + arrived[1, h, part, t].astype(F32))
                final[t, h, 2 * part:2 * part + 2] = whole.astype(BF).reshape(2, ROWS, HEAD)

            @pl.when(side == part)
            def _():
                for t in (2, 3):
                    out_copy(t, h, 1).start()
                    out_own_copy(t, h).start()

            @pl.when(side != part)
            def _():
                for t in (2, 3):
                    out_copy(t, h, 2).start()
                    out_copy(t, h, 3).start()

    def head(h, carry):
        for t in range(4):
            own_copy(t, h).wait()
            if t >= 2:
                for d in (1, 2, 3):
                    in_copy(t, h, d, False).wait_recv()
        for c in range(2):
            at = slice(2 * c, 2 * c + 2)
            qtx[h, c, :HEAD] = qs[h, at].reshape(TILE, HEAD).T
            gt[c] = gs[h, at].reshape(TILE, HEAD).T

        def window_arrival(way):
            for t in range(2):
                for d in range(4):
                    block = partner(d) + (0 if way == 0 else 2 * REACH)
                    remote(landing(t, h, block), landing(t, h, block), z_send.at[1 - way, t, h, d],
                           z_recv.at[1 - way, t, h, d], me + (-REACH if way == 0 else REACH)).wait_recv()

        def turned(i):
            vt[i] = vw[h, 2 * i:2 * i + 2].reshape(TILE, HEAD).T
            kt[i] = kx[h, 2 * i:2 * i + 2, :, :HEAD].reshape(TILE, HEAD).T

        turned(2)
        turned(3)
        both_ways(window_arrival)
        for i in (0, 1, 4, 5):
            turned(i)

        def relay_next():
            @pl.when(h == 0)
            def _():
                relay(1, 2)
                relay(1, 3)

        chunk(h, 0, relay_next)
        stage[0, h, 0] = acc[h, 0].astype(BF)
        pl.when(has_low)(lambda: gz_copy(0, h, 0).start())
        chunk(h, 1)
        stage[0, h, 1] = acc[h, 1].astype(BF)
        pl.when(has_low)(lambda: gz_copy(0, h, 1).start())
        for part in range(2):
            stage[1, h, part] = acc[h, 4 + part].astype(BF)
            pl.when(has_high)(lambda: gz_copy(1, h, part).start())
        for t in range(2):
            for d in (2, 3, 1):
                out_copy(t, h, d).start()
            out_own_copy(t, h).start()
        return carry

    lax.fori_loop(0, PAIR, head, 0)

    for h in range(PAIR):
        for t in range(4):
            for d in (1, 2, 3):
                in_copy(t, h, d, True).wait_send()

        def sent(way):
            for t in range(2):
                for d in range(4):
                    z_copy(way, t, h, d).wait_send()

        both_ways(sent)

    finish(0)
    finish(1)
    for h in range(PAIR):
        both_ways(lambda way: [gz_copy(way, h, part).wait_send() for part in range(2)] and None)
        for t in range(4):
            out_own_copy(t, h).wait()
            for d in (1, 2, 3):
                out_copy(t, h, d).wait_send()
                out_arrival(t, h, d).wait_recv()


def hand_over(*refs):
    sources, results, sems = refs[:4], refs[4:8], refs[8]
    copies = [pltpu.make_async_copy(sources[t], results[t], sems.at[t]) for t in range(4)]
    for copy in copies:
        copy.start()
    for copy in copies:
        copy.wait()


def shards(slabs, query, key, value, out_grad, session):
    rows, features = query.shape
    dma = pltpu.SemaphoreType.DMA
    result = jax.ShapeDtypeStruct((rows, features), BF)
    done = pl.pallas_call(
        functools.partial(kernel, slabs),
        out_shape=(pltpu.VMEM((rows, features), BF),) * 4,
        in_specs=[pl.BlockSpec(memory_space=pltpu.HBM)] * 4 + [pl.BlockSpec(memory_space=pltpu.VMEM)],
        out_specs=(pl.BlockSpec(memory_space=pltpu.VMEM),) * 4,
        scratch_shapes=[
            pltpu.VMEM((PAIR, 3 * REACH, ROWS, 2 * HEAD), BF),
            pltpu.VMEM((PAIR, 3 * REACH, ROWS, HEAD), BF),
            pltpu.VMEM((PAIR, REACH, ROWS, HEAD), BF),
            pltpu.VMEM((PAIR, REACH, ROWS, HEAD), BF),
            pltpu.VMEM((PAIR, 2, 2 * HEAD, TILE), BF),
            pltpu.VMEM((2, HEAD, TILE), BF),
            pltpu.VMEM((6, HEAD, TILE), BF),
            pltpu.VMEM((6, HEAD, TILE), BF),
            pltpu.VMEM((5, TILE, TILE), F32),
            pltpu.VMEM((PAIR, 6, 2, TILE, HEAD), F32),
            pltpu.VMEM((2, PAIR, 2, 2, TILE, HEAD), BF),
            pltpu.VMEM((2, PAIR, 2, 2, TILE, HEAD), BF),
            pltpu.VMEM((2, PAIR, REACH, ROWS, HEAD), BF),
            pltpu.VMEM((2, PAIR, REACH, ROWS, HEAD), BF),
            dma((4, PAIR)),
            dma((4, PAIR, 3)),
            dma((4, PAIR, 3)),
            dma((2, 2, PAIR, 4)),
            dma((2, 2, PAIR, 4)),
            dma((2, PAIR, 2)),
            dma((2, PAIR, 2)),
            dma((4, PAIR)),
            dma((4, PAIR, 3)),
            dma((4, PAIR, 3)),
        ],
        compiler_params=pltpu.CompilerParams(
            collective_id=0, has_side_effects=True, vmem_limit_bytes=62 * 1024 * 1024),
        cost_estimate=pl.CostEstimate(
            flops=2_000_000_000, bytes_accessed=2_100_000, transcendentals=1_300_000),
    )(query, key, value, out_grad, session.reshape(-1, ROWS))
    return pl.pallas_call(
        hand_over,
        out_shape=(result,) * 4,
        in_specs=[pl.BlockSpec(memory_space=pl.ANY)] * 4,
        out_specs=(pl.BlockSpec(memory_space=pltpu.HBM),) * 4,
        scratch_shapes=[dma((4,))],
        compiler_params=pltpu.CompilerParams(vmem_limit_bytes=4 * 1024 * 1024),
    )(*done)


def solution(mesh):
    split = P(("groups", "seq"), None)
    return jax.shard_map(
        functools.partial(shards, mesh.shape["seq"] // REACH),
        mesh=mesh,
        in_specs=(split, split, split, split, P("groups")),
        out_specs=(split,) * 4,
        check_vma=False,
    )
```
